256 devices in a mesh: seg: 128 (over y, x, z_lo, core), feat: 2 (over z_hi).
Axes of the slice: x: 4, y: 4, z: 8 (z_hi: 2, z_lo: 4; z = z_hi * 4 + z_lo), core: 2. Of those that a mesh axis runs over, the one named last changes fastest.
Arguments:
- train_feats: bfloat16 [65536, 8192], P('seg', 'feat'), may hold values from -24 to 24
- test_feats: bfloat16 [8192, 8192], P('seg', 'feat'), may hold values from -6 to 6
- factor_panel: bfloat16 [8192, 256], P('feat'), may hold values from -0.0625 to 0.0625
Outputs:
- gram_panel: float32 [256, 8192], P('seg', 'feat')
- scores: bfloat16 [65536, 8192], P(('seg', 'feat'))
The draws below stay inside these ranges and needn't reach their ends.
All inputs are finite; a program needn't handle non-finite values.
Results may differ from the reference program's by a relative error of at most 0.0057.
Values may be sent and summed in bfloat16 or wider, within the bound.
No kernel may reach another device: no remote copies, remote signals or barrier semaphores. Data moves between devices by JAX's collectives and lax.ppermute only.
A program may use at most 64 MiB of HBM per device.

```python
import math
import jax
import jax.numpy as jnp
from jax import lax

K = 8192
W = 256
R = 256
N_TRAIN = 65536
N_TEST = 8192


def strengthened(values, rng, source, target, shards_of, factor):
    owner, partner = [(jnp.arange(values.shape[position]) // (values.shape[position] // shards_of)).reshape([-1 if axis == position else 1 for axis in range(values.ndim)]) for position in (source, target)]
    chosen = jax.random.permutation(rng, shards_of)[partner]
    strong = (owner == chosen) | (owner == (partner + shards_of // 2) % shards_of)
    return jnp.where(strong, factor * values, values)


def block_levels(own_key, shape, shards, smallest, top_value):
    factor_of = 1.0
    for axis_at, shards_of in shards:
        draws = jax.random.uniform(jax.random.fold_in(jax.random.fold_in(own_key, 6), axis_at), (shards_of,), jnp.float32, smallest / len(shards), top_value / len(shards))
        factor_of = factor_of * jnp.repeat(jnp.exp(draws), shape[axis_at] // shards_of).reshape((-1,) + (1,) * (len(shape) - 1 - axis_at))
    return factor_of


def normal_values(stream_key, dims, scale, most, cuts=(), kind=jnp.bfloat16):
    entries = scale * jax.random.normal(stream_key, dims, jnp.float32)
    if cuts:
        entries = entries * block_levels(stream_key, dims, cuts, -0.22, 0.18)
    return jnp.clip(entries, -most, most).astype(kind)


def gaussian_with(rng, dims, scale, limit, pieces, heavy, dtype=jnp.bfloat16):
    array = scale * jax.random.normal(rng, dims, jnp.float32)
    if pieces:
        array = array * block_levels(rng, dims, pieces, -0.22, 0.18)
    return jnp.clip(strengthened(array, jax.random.fold_in(rng, 3), *heavy), -limit, limit).astype(dtype)


def setup_inputs(seed: int = 0) -> dict:
    arg_keys = jax.random.split(jax.random.key(seed), 4)
    train_feats = gaussian_with(arg_keys[0], (N_TRAIN, K), 1.0, 24.0, ((0, 128), (1, 2)), (0, 1, 128, 5.5))
    test_feats = normal_values(arg_keys[1], (N_TEST, K), 1.0, 6.0, ((0, 128), (1, 2)))
    factor_panel = normal_values(arg_keys[2], (K, R), K ** -0.5, 0.0625, ((0, 2),))
    return dict(train_feats=train_feats, test_feats=test_feats, factor_panel=factor_panel)


def reference(train_feats, test_feats, factor_panel):
    n_train = train_feats.shape[0]
    panel_cols = train_feats[:, :W]
    gram_panel = lax.dot_general(panel_cols, train_feats, (((0,), (0,)), ((), ())), preferred_element_type=jnp.float32) / n_train
    proj_test = jnp.dot(test_feats, factor_panel, preferred_element_type=jnp.float32).astype(jnp.bfloat16)
    scale = 1.0 / math.sqrt(R)
    blocks = train_feats.reshape(n_train // 1024, 1024, train_feats.shape[1]) if n_train % 1024 == 0 else train_feats.reshape(1, n_train, train_feats.shape[1])

    def one_block(rows):
        proj_rows = jnp.dot(rows, factor_panel, preferred_element_type=jnp.float32).astype(jnp.bfloat16)
        block_scores = lax.dot_general(proj_rows, proj_test, (((1,), (1,)), ((), ())), preferred_element_type=jnp.float32)
        return (block_scores * scale).astype(jnp.bfloat16)
    scores = lax.map(one_block, blocks).reshape(n_train, proj_test.shape[0])
    return (gram_panel, scores)
```

```python
import math

import jax
import jax.numpy as jnp
from jax import lax
from jax.experimental import pallas as pl
from jax.experimental.pallas import tpu as pltpu
from jax.sharding import Mesh, PartitionSpec as P

W = 256
AXES = ("y", "x", "l", "c", "h")
SIZES = (4, 4, 4, 2, 2)
VMEM = 48 * 1024 * 1024


def pairs(move, keep=None):
    out = []
    for i in range(math.prod(SIZES)):
        h, c, l, yx = i % 2, i // 2 % 2, i // 4 % 4, i // 16
        if keep is None or keep(l, c, h):
            l2, c2, h2 = move(l, c, h)
            out.append((i, ((yx * 4 + l2) * 2 + c2) * 2 + h2))
    return out


OTHER_HALF = pairs(lambda l, c, h: (l, c, 1 - h))
TO_SECOND_HALF = pairs(lambda l, c, h: (l, c, 1), lambda l, c, h: h == 0)
OTHER_CORE = pairs(lambda l, c, h: (l, 1 - c, h))
ALONG = [pairs(lambda l, c, h, d=d: ((l + d) % 4, c, h)) for d in range(4)]


def pack_kernel(mine_ref, got_ref, proj_ref, out_ref):
    both = mine_ref[...] + got_ref[...].astype(jnp.float32)
    for dest in range(2):
        out_ref[dest, :256, :] = proj_ref[...]
        rows = both[8 * dest : 8 * dest + 8, :]
        for p in range(8):
            two = jnp.concatenate(
                [rows[:, 512 * p : 512 * p + 256], rows[:, 512 * p + 256 : 512 * p + 512]], axis=0
            )
            out_ref[dest, 256 + 16 * p : 272 + 16 * p, :] = two.astype(jnp.bfloat16)


def pack(mine, got, proj):
    return pl.pallas_call(
        pack_kernel,
        grid=(8,),
        in_specs=[
            pl.BlockSpec((16, 4096), lambda i: (i, 0)),
            pl.BlockSpec((16, 4096), lambda i: (i, 0)),
            pl.BlockSpec((256, 256), lambda i: (0, 0)),
        ],
        out_specs=pl.BlockSpec((2, 384, 256), lambda i: (i, 0, 0)),
        out_shape=jax.ShapeDtypeStruct((16, 384, 256), jnp.bfloat16),
        compiler_params=pltpu.CompilerParams(vmem_limit_bytes=VMEM),
        cost_estimate=pl.CostEstimate(flops=524288, bytes_accessed=6 << 20, transcendentals=0),
        name="pack",
    )(mine, got, proj)


def fold_kernel(in_ref, own_ref, a_ref, b_ref, d_ref, sum_ref):
    total = in_ref[0].astype(jnp.float32)
    for s in range(1, 16):
        total = total + in_ref[s].astype(jnp.float32)
    sum_ref[0] = total[:, :128]
    sum_ref[1] = total[:, 128:]
    for step, ref in enumerate((own_ref, a_ref, b_ref, d_ref)):
        for j in range(2):
            for half in range(2):
                rows = sum_ref[half, pl.ds(2 * step + j, 16, stride=8), :]
                ref[16 * j : 16 * j + 16, 128 * half : 128 * half + 128] = rows.astype(ref.dtype)


def fold(merged):
    whole = pl.BlockSpec((32, 256), lambda i: (0, 0))
    return pl.pallas_call(
        fold_kernel,
        grid=(1,),
        in_specs=[pl.BlockSpec((16, 128, 256), lambda i: (0, 2, 0))],
        out_specs=[whole] * 4,
        out_shape=[jax.ShapeDtypeStruct((32, 256), jnp.float32)]
        + [jax.ShapeDtypeStruct((32, 256), jnp.bfloat16)] * 3,
        scratch_shapes=[pltpu.VMEM((2, 128, 128), jnp.float32)],
        compiler_params=pltpu.CompilerParams(vmem_limit_bytes=VMEM),
        cost_estimate=pl.CostEstimate(flops=524288, bytes_accessed=1 << 20, transcendentals=0),
        name="fold",
    )(merged)


def scores_kernel(core_ref, train_ref, own_ref, other_ref, out_ref, both_ref):
    core = core_ref[0]
    for s in range(2):
        for l in range(4):
            base = 512 * s + 128 * l
            mine = pl.multiple_of(base + 64 * core, 64)
            theirs = pl.multiple_of(base + 64 * (1 - core), 64)
            both_ref[pl.ds(mine, 64), :] = own_ref[s, 64 * l : 64 * l + 64, :]
            both_ref[pl.ds(theirs, 64), :] = other_ref[s, 64 * l : 64 * l + 64, :]
    product = lax.dot_general(
        train_ref[...], both_ref[...], (((1,), (1,)), ((), ())), preferred_element_type=jnp.float32
    )
    out_ref[...] = (product * (1.0 / math.sqrt(256))).astype(jnp.bfloat16)


def scores_of(core, proj_train, own, other):
    return pl.pallas_call(
        scores_kernel,
        grid_spec=pltpu.PrefetchScalarGridSpec(
            num_scalar_prefetch=1,
            grid=(8,),
            in_specs=[
                pl.BlockSpec((256, 256), lambda i, c: (0, 0)),
                pl.BlockSpec((2, 256, 256), lambda i, c: (i, 0, 0)),
                pl.BlockSpec((2, 256, 256), lambda i, c: (i, 0, 0)),
            ],
            out_specs=pl.BlockSpec((256, 1024), lambda i, c: (0, i)),
            scratch_shapes=[pltpu.VMEM((1024, 256), jnp.bfloat16)],
        ),
        out_shape=jax.ShapeDtypeStruct((256, 8192), jnp.bfloat16),
        compiler_params=pltpu.CompilerParams(vmem_limit_bytes=VMEM),
        cost_estimate=pl.CostEstimate(flops=1 << 30, bytes_accessed=8 << 20, transcendentals=0),
        name="scores",
    )(core, proj_train, own, other)


def local(train_feats, test_feats, factor_panel):
    f32, bf16 = jnp.float32, jnp.bfloat16
    l, c, h = lax.axis_index("l"), lax.axis_index("c"), lax.axis_index("h")

    first = train_feats[:, :W]
    panel = jnp.where(h == 0, first, lax.ppermute(first, AXES, TO_SECOND_HALF))
    place = jnp.arange(W)
    core_of, yx_of, step_of, j_of = place // 128, place // 8 % 16, place // 2 % 4, place % 2
    column = ((yx_of * 4 + (l + step_of) % 4) * 2 + (c + core_of) % 2) * 2 + j_of
    choose = (jnp.arange(W)[:, None] == column[None, :]).astype(bf16)
    ordered = jnp.dot(panel, choose, preferred_element_type=f32).astype(bf16)
    term = lax.dot_general(ordered, train_feats, (((0,), (0,)), ((), ())), preferred_element_type=f32)
    got = lax.ppermute(term[128:].astype(bf16), AXES, OTHER_CORE)

    part = jnp.dot(test_feats, factor_panel, preferred_element_type=f32).astype(bf16)
    parts = lax.all_to_all(jnp.broadcast_to(part, (8, 64, 256)), ("h", "l"), 0, 0, tiled=True)
    parts = parts.reshape(2, 256, 256).astype(f32)
    proj_test = (parts[0] + parts[1]).astype(bf16)

    merged = lax.all_to_all(pack(term[:128], got, proj_test), ("y", "x"), 0, 0, tiled=True)

    own, *sent = fold(merged)
    total = own
    for d, block in enumerate(sent, 1):
        total = total + lax.ppermute(block, AXES, ALONG[d]).astype(f32)
    gram_panel = total.reshape(2, 4096) / 65536

    train_part = jnp.dot(train_feats, factor_panel, preferred_element_type=f32)
    keep = lax.dynamic_slice_in_dim(train_part, h * 256, 256)
    give = lax.dynamic_slice_in_dim(train_part, (1 - h) * 256, 256)
    proj_train = (keep + lax.ppermute(give, AXES, OTHER_HALF)).astype(bf16)
    gathered = merged[:, :256, :]
    other = lax.ppermute(gathered, AXES, OTHER_CORE)
    scores = scores_of(c.astype(jnp.int32)[None], proj_train, gathered, other)
    return (gram_panel, scores)


def solution(mesh):
    fine = Mesh(mesh.devices.reshape(SIZES), AXES)
    seg = ("y", "x", "l", "c")
    in_specs = (P(seg, "h"), P(seg, "h"), P("h", None))
    out_specs = (P(seg, "h"), P((*seg, "h"), None))
    return jax.shard_map(local, mesh=fine, in_specs=in_specs, out_specs=out_specs, check_vma=False)
```

```python
import math

import jax
import jax.numpy as jnp
from jax import lax
from jax.experimental import pallas as pl
from jax.experimental.pallas import tpu as pltpu
from jax.sharding import Mesh, PartitionSpec as P

W = 256
AXES = ("y", "x", "l", "c", "h")
SIZES = (4, 4, 4, 2, 2)
MIB = 1 << 20
BIG = 56
BF16, F32 = jnp.bfloat16, jnp.float32


def pairs(move, keep=None):
    out = []
    for i in range(math.prod(SIZES)):
        h, c, l, yx = i % 2, i // 2 % 2, i // 4 % 4, i // 16
        if keep is None or keep(l, c, h):
            l2, c2, h2 = move(l, c, h)
            out.append((i, ((yx * 4 + l2) * 2 + c2) * 2 + h2))
    return out


OTHER_HALF = pairs(lambda l, c, h: (l, c, 1 - h))
TO_SECOND_HALF = pairs(lambda l, c, h: (l, c, 1), lambda l, c, h: h == 0)
OTHER_CORE = pairs(lambda l, c, h: (l, 1 - c, h))
ALONG = [pairs(lambda l, c, h, d=d: ((l + d) % 4, c, h)) for d in range(4)]


def params(mib):
    return pltpu.CompilerParams(vmem_limit_bytes=mib * MIB)


def cost(flops, nbytes):
    return pl.CostEstimate(flops=flops, bytes_accessed=nbytes, transcendentals=0)


def anywhere():
    return pl.BlockSpec(memory_space=pltpu.HBM)


def whole():
    return pl.BlockSpec(memory_space=pltpu.VMEM)


def test_kernel(test_ref, factor_ref, after_ref, out_ref, held_ref, test_vmem, sem):
    del after_ref
    copies = []
    for k in range(4):
        part = pl.ds(1024 * k, 1024)
        copies.append(pltpu.make_async_copy(factor_ref.at[part, :], held_ref.at[part, :], sem.at[2 * k]))
        copies.append(
            pltpu.make_async_copy(test_ref.at[:, part], test_vmem.at[:, part], sem.at[2 * k + 1])
        )
    for copy in copies:
        copy.start()
    total = jnp.zeros((64, 256), F32)
    for k in range(4):
        copies[2 * k].wait()
        copies[2 * k + 1].wait()
        total += jnp.dot(
            test_vmem[:, 1024 * k : 1024 * k + 1024],
            held_ref[1024 * k : 1024 * k + 1024, :],
            preferred_element_type=F32,
        )
    part = total.astype(BF16)
    for dest in range(16):
        out_ref[dest] = part[:, 128 * (dest % 2) : 128 * (dest % 2) + 128]


def test_parts(test_feats, factor_panel, after):
    return pl.pallas_call(
        test_kernel,
        in_specs=[anywhere()] * 3,
        out_specs=[whole()] * 2,
        out_shape=[
            jax.ShapeDtypeStruct((16, 64, 128), BF16),
            jax.ShapeDtypeStruct((4096, 256), BF16),
        ],
        scratch_shapes=[pltpu.VMEM((64, 4096), BF16), pltpu.SemaphoreType.DMA((8,))],
        compiler_params=params(8),
        cost_estimate=cost(2 * 64 * 4096 * 256, 5 * MIB),
        name="test_parts",
    )(test_feats, factor_panel, after)


def gram_kernel(at_ref, got_ref, train_ref, mine_ref, theirs_ref):
    l, c, h = at_ref[0], at_ref[1], at_ref[2]
    place = lax.broadcasted_iota(jnp.int32, (256, 256), 0)
    column = lax.broadcasted_iota(jnp.int32, (256, 256), 1)
    yx, l_of, c_of = (place >> 1) & 15, (l + (place >> 5)) & 3, (c + (place >> 7)) & 1
    wanted = (yx << 4) + (l_of << 2) + (c_of << 1) + (place & 1)
    choose = jnp.where(wanted == column, 1.0, 0.0).astype(BF16)
    panel = jnp.where(h == 0, train_ref[:, :W].astype(F32), got_ref[...].astype(F32)).astype(BF16)
    panel = lax.dot_general(choose, panel, (((1,), (1,)), ((), ())), preferred_element_type=F32)
    panel = panel.astype(BF16)
    for i in range(8):
        term = jnp.dot(panel, train_ref[:, 512 * i : 512 * i + 512], preferred_element_type=F32)
        blocks = [term[:, 128 * t : 128 * t + 128].reshape(32, 8, 128) for t in range(4)]
        term = jnp.concatenate(blocks, axis=1)
        mine_ref[:, 32 * i : 32 * i + 32, :] = term[:16]
        theirs_ref[:, 32 * i : 32 * i + 32, :] = term[16:].astype(BF16)


def gram_terms(at, got, train_feats):
    return pl.pallas_call(
        gram_kernel,
        in_specs=[pl.BlockSpec(memory_space=pltpu.SMEM), whole(), whole()],
        out_specs=[whole()] * 2,
        out_shape=[
            jax.ShapeDtypeStruct((16, 256, 128), F32),
            jax.ShapeDtypeStruct((16, 256, 128), BF16),
        ],
        compiler_params=params(16),
        cost_estimate=cost(2 * 256 * 512 * 4096, 7 * MIB),
        name="gram_terms",
    )(at, got, train_feats)


def spread_kernel(parts_ref, out_ref, proj_ref):
    @pl.when(pl.program_id(0) == 0)
    def _():
        proj = (parts_ref[:8].astype(F32) + parts_ref[8:].astype(F32)).reshape(4, 128, 128)
        for l in range(4):
            proj_ref[128 * l : 128 * l + 128, :] = proj[l].T.astype(BF16)

    for dest in range(4):
        out_ref[dest] = proj_ref[...]


def spread(parts):
    return pl.pallas_call(
        spread_kernel,
        grid=(4,),
        in_specs=[pl.BlockSpec((16, 64, 128), lambda i: (0, 0, 0))],
        out_specs=pl.BlockSpec((4, 512, 128), lambda i: (i, 0, 0)),
        out_shape=jax.ShapeDtypeStruct((16, 512, 128), BF16),
        scratch_shapes=[pltpu.VMEM((512, 128), BF16)],
        compiler_params=params(BIG),
        cost_estimate=cost(MIB, 2 * MIB),
        name="spread",
    )(parts)


def cores_kernel(mine_ref, got_ref, own_ref, a_ref, b_ref, d_ref):
    own_ref[...] = mine_ref[:4] + got_ref[:4].astype(F32)
    for step, ref in enumerate((a_ref, b_ref, d_ref), 1):
        rows = slice(4 * step, 4 * step + 4)
        ref[...] = (mine_ref[rows] + got_ref[rows].astype(F32)).astype(BF16)


def sum_cores(mine, got):
    return pl.pallas_call(
        cores_kernel,
        in_specs=[whole()] * 2,
        out_specs=[whole()] * 4,
        out_shape=[jax.ShapeDtypeStruct((4, 256, 128), F32)]
        + [jax.ShapeDtypeStruct((4, 256, 128), BF16)] * 3,
        compiler_params=params(8),
        cost_estimate=cost(MIB // 2, 4 * MIB),
        name="sum_cores",
    )(mine, got)


def line_kernel(own_ref, a_ref, b_ref, d_ref, out_ref, sum_ref):
    sum_ref[...] = own_ref[...] + a_ref[...].astype(F32) + b_ref[...].astype(F32) + d_ref[...].astype(F32)
    for yx in range(16):
        for j in range(2):
            rows = sum_ref[yx // 4, pl.ds(2 * (yx % 4) + j, 32, stride=8), :]
            out_ref[yx, 32 * j : 32 * j + 32, :] = rows.astype(BF16)


def sum_line(own, sums):
    return pl.pallas_call(
        line_kernel,
        in_specs=[whole()] * 4,
        out_specs=whole(),
        out_shape=jax.ShapeDtypeStruct((16, 64, 128), BF16),
        scratch_shapes=[pltpu.VMEM((4, 256, 128), F32)],
        compiler_params=params(8),
        cost_estimate=cost(MIB // 2, 2 * MIB),
        name="sum_line",
    )(own, *sums)


def plane_kernel(in_ref, out_ref):
    total = in_ref[0].astype(F32)
    for s in range(1, 16):
        total = total + in_ref[s].astype(F32)
    out_ref[...] = total / 65536


def sum_plane(rows):
    return pl.pallas_call(
        plane_kernel,
        in_specs=[whole()],
        out_specs=whole(),
        out_shape=jax.ShapeDtypeStruct((64, 128), F32),
        compiler_params=params(8),
        cost_estimate=cost(MIB // 8, MIB // 4),
        name="sum_plane",
    )(rows)


def train_kernel(at_ref, train_ref, factor_ref, keep_ref, give_ref, held_ref, sum_ref, sem):
    copies = []
    for k in range(8):
        part = pl.ds(512 * k, 512)
        copies.append(pltpu.make_async_copy(train_ref.at[:, part], held_ref.at[:, part], sem.at[k]))
    for copy in copies:
        copy.start()
    sum_ref[...] = jnp.zeros_like(sum_ref)
    for k in range(4):
        copies[2 * k].wait()
        copies[2 * k + 1].wait()
        part = slice(1024 * k, 1024 * k + 1024)
        sum_ref[...] += jnp.dot(held_ref[:, part], factor_ref[part, :], preferred_element_type=F32)
    h = at_ref[2]
    keep_ref[...] = sum_ref[pl.ds(pl.multiple_of(256 * h, 256), 256), :]
    give_ref[...] = sum_ref[pl.ds(pl.multiple_of(256 - 256 * h, 256), 256), :].astype(BF16)


def train_parts(at, train_feats, factor_panel):
    return pl.pallas_call(
        train_kernel,
        in_specs=[pl.BlockSpec(memory_space=pltpu.SMEM), anywhere(), whole()],
        out_specs=[whole()] * 3,
        out_shape=[
            jax.ShapeDtypeStruct((256, 256), F32),
            jax.ShapeDtypeStruct((256, 256), BF16),
            jax.ShapeDtypeStruct((512, 4096), BF16),
        ],
        scratch_shapes=[pltpu.VMEM((512, 256), F32), pltpu.SemaphoreType.DMA((8,))],
        compiler_params=params(12),
        cost_estimate=cost(2 * 512 * 4096 * 256, 9 * MIB),
        name="train_parts",
    )(at, train_feats, factor_panel)


def scores_kernel(at_ref, keep_ref, got_ref, own_ref, other_ref, out_ref, proj_ref):
    i = pl.program_id(0)

    @pl.when(i == 0)
    def _():
        c = at_ref[1]
        proj = keep_ref[...] + got_ref[...].astype(F32)
        low, high = proj[:, :128], proj[:, 128:]
        proj_ref[:, :128] = jnp.where(c == 0, low, high).astype(BF16)
        proj_ref[:, 128:] = jnp.where(c == 0, high, low).astype(BF16)

    for n in range(4):
        at = 2 * i + n // 2
        tests = jnp.concatenate(
            [
                jnp.concatenate(
                    [ref[at, 256 * (n % 2) + 128 * t : 256 * (n % 2) + 128 * t + 128, :] for t in range(2)],
                    axis=1,
                )
                for ref in (own_ref, other_ref)
            ],
            axis=0,
        )
        product = jnp.dot(proj_ref[...], tests, preferred_element_type=F32)
        out_ref[:, 256 * n : 256 * n + 256] = (product * (1.0 / math.sqrt(256))).astype(BF16)


def scores_of(at, keep, got, own, other):
    return pl.pallas_call(
        scores_kernel,
        grid=(8,),
        in_specs=[pl.BlockSpec(memory_space=pltpu.SMEM)] + [whole()] * 4,
        out_specs=pl.BlockSpec((256, 1024), lambda i: (0, i)),
        out_shape=jax.ShapeDtypeStruct((256, 8192), BF16),
        scratch_shapes=[pltpu.VMEM((256, 256), BF16)],
        compiler_params=params(12),
        cost_estimate=cost(1 << 30, 8 * MIB),
        name="scores",
    )(at, keep, got, own, other)


def local(train_feats, test_feats, factor_panel):
    at = jnp.stack([lax.axis_index(a) for a in ("l", "c", "h")]).astype(jnp.int32)

    first = train_feats[:, :W]
    sent = lax.ppermute(first, AXES, TO_SECOND_HALF)
    part, factor = test_parts(test_feats, factor_panel, first)
    parts = lax.all_to_all(part, ("h", "l", "c"), 0, 0, tiled=True)
    keep, give, train = train_parts(at, train_feats, factor)
    parts, sent, give = lax.optimization_barrier((parts, sent, give))
    got = lax.ppermute(give, AXES, OTHER_HALF)
    tests = spread(parts)

    sent, _ = lax.optimization_barrier((sent, tests))
    mine, theirs = gram_terms(at, sent, train)
    own, *sums = sum_cores(mine, lax.ppermute(theirs, AXES, OTHER_CORE))
    sums = [lax.ppermute(rows, AXES, ALONG[d]) for d, rows in enumerate(sums, 1)]
    rows = sum_line(own, sums)
    tests = lax.all_to_all(tests, ("y", "x"), 0, 0, tiled=True)
    tests, rows, got = lax.optimization_barrier((tests, rows, got))

    other = lax.ppermute(tests, AXES, OTHER_CORE)
    rows = lax.all_to_all(rows, ("y", "x"), 0, 0, tiled=True)
    scores = scores_of(at, keep, got, tests, other)
    rows, scores = lax.optimization_barrier((rows, scores))
    gram_panel = sum_plane(rows).reshape(2, 4096)
    return (gram_panel, scores)


def solution(mesh):
    fine = Mesh(mesh.devices.reshape(SIZES), AXES)
    seg = ("y", "x", "l", "c")
    in_specs = (P(seg, "h"), P(seg, "h"), P("h", None))
    out_specs = (P(seg, "h"), P((*seg, "h"), None))
    return jax.shard_map(local, mesh=fine, in_specs=in_specs, out_specs=out_specs, check_vma=False)
```

```python
import math

import jax
import jax.numpy as jnp
from jax import lax
from jax.experimental import pallas as pl
from jax.experimental.pallas import tpu as pltpu
from jax.sharding import Mesh, PartitionSpec as P

W = 256
AXES = ("y", "x", "l", "c", "h")
SIZES = (4, 4, 4, 2, 2)
MIB = 1 << 20
BIG = 56
BF16, F32 = jnp.bfloat16, jnp.float32


def pairs(move, keep=None):
    out = []
    for i in range(math.prod(SIZES)):
        h, c, l, yx = i % 2, i // 2 % 2, i // 4 % 4, i // 16
        if keep is None or keep(l, c, h):
            l2, c2, h2 = move(l, c, h)
            out.append((i, ((yx * 4 + l2) * 2 + c2) * 2 + h2))
    return out


OTHER_HALF = pairs(lambda l, c, h: (l, c, 1 - h))
TO_SECOND_HALF = pairs(lambda l, c, h: (l, c, 1), lambda l, c, h: h == 0)
OTHER_CORE = pairs(lambda l, c, h: (l, 1 - c, h))
ALONG = [pairs(lambda l, c, h, d=d: ((l + d) % 4, c, h)) for d in range(4)]


def params(mib):
    return pltpu.CompilerParams(vmem_limit_bytes=mib * MIB)


def cost(flops, nbytes):
    return pl.CostEstimate(flops=flops, bytes_accessed=nbytes, transcendentals=0)


def anywhere():
    return pl.BlockSpec(memory_space=pltpu.HBM)


def whole():
    return pl.BlockSpec(memory_space=pltpu.VMEM)


def test_kernel(test_ref, factor_ref, keep_ref, give_ref):
    total = jnp.dot(test_ref[...], factor_ref[...], preferred_element_type=F32)
    keep_ref[...] = total
    give_ref[...] = total.astype(BF16)


def test_parts(test_feats, factor_panel):
    return pl.pallas_call(
        test_kernel,
        in_specs=[whole()] * 2,
        out_specs=[whole()] * 2,
        out_shape=[jax.ShapeDtypeStruct((64, 256), F32), jax.ShapeDtypeStruct((64, 256), BF16)],
        compiler_params=params(8),
        cost_estimate=cost(2 * 64 * 4096 * 256, 3 * MIB),
        name="test_parts",
    )(test_feats, factor_panel)


def gram_kernel(at_ref, got_ref, train_ref, mine_ref, theirs_ref):
    l, c, h = at_ref[0], at_ref[1], at_ref[2]
    place = lax.broadcasted_iota(jnp.int32, (256, 256), 0)
    column = lax.broadcasted_iota(jnp.int32, (256, 256), 1)
    yx, l_of, c_of = (place >> 3) & 15, (l + (place >> 1)) & 3, (c + (place >> 7)) & 1
    wanted = (yx << 4) + (l_of << 2) + (c_of << 1) + (place & 1)
    choose = jnp.where(wanted == column, 1.0, 0.0).astype(BF16)
    panel = jnp.where(h == 0, train_ref[:, :W].astype(F32), got_ref[...].astype(F32)).astype(BF16)
    panel = lax.dot_general(choose, panel, (((1,), (1,)), ((), ())), preferred_element_type=F32)
    panel = panel.astype(BF16)
    for i in range(8):
        term = jnp.dot(panel, train_ref[:, 512 * i : 512 * i + 512], preferred_element_type=F32)
        blocks = [term[:, 128 * t : 128 * t + 128].reshape(32, 8, 128) for t in range(4)]
        term = jnp.concatenate(blocks, axis=1)
        mine_ref[:, 32 * i : 32 * i + 32, :] = term[:16]
        theirs_ref[:, 32 * i : 32 * i + 32, :] = term[16:].astype(BF16)


def gram_terms(at, got, train_feats):
    return pl.pallas_call(
        gram_kernel,
        in_specs=[pl.BlockSpec(memory_space=pltpu.SMEM), whole(), whole()],
        out_specs=[whole()] * 2,
        out_shape=[
            jax.ShapeDtypeStruct((16, 256, 128), F32),
            jax.ShapeDtypeStruct((16, 256, 128), BF16),
        ],
        compiler_params=params(16),
        cost_estimate=cost(2 * 256 * 512 * 4096, 7 * MIB),
        name="gram_terms",
    )(at, got, train_feats)


def halves_kernel(keep_ref, got_ref, out_ref):
    proj = (keep_ref[...] + got_ref[...].astype(F32)).astype(BF16)
    for dest in range(8):
        out_ref[dest] = proj[:, 128 * (dest % 2) : 128 * (dest % 2) + 128]


def sum_halves(keep, got):
    return pl.pallas_call(
        halves_kernel,
        in_specs=[whole()] * 2,
        out_specs=whole(),
        out_shape=jax.ShapeDtypeStruct((8, 64, 128), BF16),
        compiler_params=params(8),
        cost_estimate=cost(1 << 16, MIB // 4),
        name="sum_halves",
    )(keep, got)


def spread_kernel(parts_ref, out_ref):
    proj = parts_ref[...].astype(F32).reshape(4, 128, 128)
    proj = jnp.concatenate([proj[l].T for l in range(4)], axis=0).astype(BF16)
    for dest in range(16):
        out_ref[dest] = proj


def spread(parts):
    return pl.pallas_call(
        spread_kernel,
        in_specs=[whole()],
        out_specs=whole(),
        out_shape=jax.ShapeDtypeStruct((16, 512, 128), BF16),
        compiler_params=params(8),
        cost_estimate=cost(MIB, 2 * MIB),
        name="spread",
    )(parts)


def cores_kernel(mine_ref, got_ref, out_ref):
    out_ref[...] = (mine_ref[...] + got_ref[...].astype(F32)).astype(BF16)


def sum_cores(mine, got):
    return pl.pallas_call(
        cores_kernel,
        in_specs=[whole()] * 2,
        out_specs=whole(),
        out_shape=jax.ShapeDtypeStruct((16, 256, 128), BF16),
        compiler_params=params(8),
        cost_estimate=cost(MIB // 2, 4 * MIB),
        name="sum_cores",
    )(mine, got)


def fold_kernel(in_ref, own_ref, a_ref, b_ref, d_ref, sum_ref):
    total = in_ref[0].astype(F32)
    for s in range(1, 16):
        total = total + in_ref[s].astype(F32)
    sum_ref[...] = total
    for step, ref in enumerate((own_ref, a_ref, b_ref, d_ref)):
        for j in range(2):
            rows = sum_ref[pl.ds(2 * step + j, 32, stride=8), :]
            ref[32 * j : 32 * j + 32, :] = rows.astype(ref.dtype)


def fold(rows):
    return pl.pallas_call(
        fold_kernel,
        in_specs=[whole()],
        out_specs=[whole()] * 4,
        out_shape=[jax.ShapeDtypeStruct((64, 128), F32)] + [jax.ShapeDtypeStruct((64, 128), BF16)] * 3,
        scratch_shapes=[pltpu.VMEM((256, 128), F32)],
        compiler_params=params(8),
        cost_estimate=cost(MIB // 2, MIB),
        name="fold",
    )(rows)


def train_kernel(at_ref, train_ref, factor_ref, keep_ref, give_ref, sum_ref):
    for n in range(4):
        rows = slice(128 * n, 128 * n + 128)
        sum_ref[rows, :] = jnp.dot(train_ref[rows, :], factor_ref[...], preferred_element_type=F32)
    h = at_ref[2]
    keep_ref[...] = sum_ref[pl.ds(pl.multiple_of(256 * h, 256), 256), :]
    give_ref[...] = sum_ref[pl.ds(pl.multiple_of(256 - 256 * h, 256), 256), :].astype(BF16)


def train_parts(at, train_feats, factor_panel):
    return pl.pallas_call(
        train_kernel,
        in_specs=[pl.BlockSpec(memory_space=pltpu.SMEM), whole(), whole()],
        out_specs=[whole()] * 2,
        out_shape=[jax.ShapeDtypeStruct((256, 256), F32), jax.ShapeDtypeStruct((256, 256), BF16)],
        scratch_shapes=[pltpu.VMEM((512, 256), F32)],
        compiler_params=params(8),
        cost_estimate=cost(2 * 512 * 4096 * 256, 7 * MIB),
        name="train_parts",
    )(at, train_feats, factor_panel)


def scores_kernel(at_ref, keep_ref, got_ref, own_ref, other_ref, out_ref, made_ref, sem):
    c = at_ref[1]
    proj = keep_ref[...] + got_ref[...].astype(F32)
    low, high = proj[:, :128], proj[:, 128:]
    proj = jnp.concatenate([jnp.where(c == 0, low, high), jnp.where(c == 0, high, low)], axis=1)
    proj = proj.astype(BF16)
    copies = []
    for n in range(32):
        tests = jnp.concatenate(
            [
                jnp.concatenate(
                    [
                        ref[n // 2, 256 * (n % 2) + 128 * t : 256 * (n % 2) + 128 * t + 128, :]
                        for t in range(2)
                    ],
                    axis=1,
                )
                for ref in (own_ref, other_ref)
            ],
            axis=0,
        )
        product = jnp.dot(proj, tests, preferred_element_type=F32)
        made_ref[:, 256 * n : 256 * n + 256] = (product * (1.0 / math.sqrt(256))).astype(BF16)
        if n % 4 == 3:
            done = pl.ds(256 * (n - 3), 1024)
            copies.append(
                pltpu.make_async_copy(made_ref.at[:, done], out_ref.at[:, done], sem.at[n // 4])
            )
            copies[-1].start()
    for copy in copies:
        copy.wait()


def scores_of(at, keep, got, own, other):
    return pl.pallas_call(
        scores_kernel,
        in_specs=[pl.BlockSpec(memory_space=pltpu.SMEM)] + [whole()] * 4,
        out_specs=anywhere(),
        out_shape=jax.ShapeDtypeStruct((256, 8192), BF16),
        scratch_shapes=[pltpu.VMEM((256, 8192), BF16), pltpu.SemaphoreType.DMA((8,))],
        compiler_params=params(16),
        cost_estimate=cost(1 << 30, 8 * MIB),
        name="scores",
    )(at, keep, got, own, other)


def local(train_feats, test_feats, factor_panel):
    at = jnp.stack([lax.axis_index(a) for a in ("l", "c", "h")]).astype(jnp.int32)

    test_keep, test_give = test_parts(test_feats, factor_panel)
    parts = sum_halves(test_keep, lax.ppermute(test_give, AXES, OTHER_HALF))
    keep, give = train_parts(at, train_feats, factor_panel)
    parts, give = lax.optimization_barrier((parts, give))
    parts = lax.all_to_all(parts, ("l", "c"), 0, 0, tiled=True)
    parts, first = lax.optimization_barrier((parts, train_feats[:, :W]))
    tests = spread(parts)

    sent = lax.ppermute(first, AXES, TO_SECOND_HALF)
    sent, give, _ = lax.optimization_barrier((sent, give, tests))
    got = lax.ppermute(give, AXES, OTHER_HALF)
    mine, theirs = gram_terms(at, sent, train_feats)
    rows = sum_cores(mine, lax.ppermute(theirs, AXES, OTHER_CORE))
    tests = lax.all_to_all(tests, ("y", "x"), 0, 0, tiled=True)
    tests, rows, got = lax.optimization_barrier((tests, rows, got))

    other = lax.ppermute(tests, AXES, OTHER_CORE)
    rows = lax.all_to_all(rows, ("y", "x"), 0, 0, tiled=True)
    scores = scores_of(at, keep, got, tests, other)
    rows, scores = lax.optimization_barrier((rows, scores))
    total, *sums = fold(rows)
    for d, block in enumerate(sums, 1):
        total = total + lax.ppermute(block, AXES, ALONG[d]).astype(F32)
    gram_panel = total.reshape(2, 4096) / 65536
    return (gram_panel, scores)


def solution(mesh):
    fine = Mesh(mesh.devices.reshape(SIZES), AXES)
    seg = ("y", "x", "l", "c")
    in_specs = (P(seg, "h"), P(seg, "h"), P("h", None))
    out_specs = (P(seg, "h"), P((*seg, "h"), None))
    return jax.shard_map(local, mesh=fine, in_specs=in_specs, out_specs=out_specs, check_vma=False)
```

```python
import math

import jax
import jax.numpy as jnp
from jax import lax
from jax.experimental import pallas as pl
from jax.experimental.pallas import tpu as pltpu
from jax.sharding import Mesh, PartitionSpec as P

W = 256
AXES = ("y", "x", "l", "c", "h")
SIZES = (4, 4, 4, 2, 2)
MIB = 1 << 20
BIG = 56
BF16, F32 = jnp.bfloat16, jnp.float32


def pairs(move, keep=None):
    out = []
    for i in range(math.prod(SIZES)):
        h, c, l, yx = i % 2, i // 2 % 2, i // 4 % 4, i // 16
        if keep is None or keep(l, c, h):
            l2, c2, h2 = move(l, c, h)
            out.append((i, ((yx * 4 + l2) * 2 + c2) * 2 + h2))
    return out


OTHER_HALF = pairs(lambda l, c, h: (l, c, 1 - h))
TO_SECOND_HALF = pairs(lambda l, c, h: (l, c, 1), lambda l, c, h: h == 0)
OTHER_CORE = pairs(lambda l, c, h: (l, 1 - c, h))
ALONG = [pairs(lambda l, c, h, d=d: ((l + d) % 4, c, h)) for d in range(4)]


def params(mib):
    return pltpu.CompilerParams(vmem_limit_bytes=mib * MIB)


def cost(flops, nbytes):
    return pl.CostEstimate(flops=flops, bytes_accessed=nbytes, transcendentals=0)


def anywhere():
    return pl.BlockSpec(memory_space=pltpu.HBM)


def whole():
    return pl.BlockSpec(memory_space=pltpu.VMEM)


def test_kernel(test_ref, factor_ref, keep_ref, give_ref):
    total = jnp.dot(test_ref[...], factor_ref[...], preferred_element_type=F32)
    keep_ref[...] = total
    give_ref[...] = total.astype(BF16)


def test_parts(test_feats, factor_panel):
    return pl.pallas_call(
        test_kernel,
        in_specs=[whole()] * 2,
        out_specs=[whole()] * 2,
        out_shape=[jax.ShapeDtypeStruct((64, 256), F32), jax.ShapeDtypeStruct((64, 256), BF16)],
        compiler_params=params(8),
        cost_estimate=cost(2 * 64 * 4096 * 256, 3 * MIB),
        name="test_parts",
    )(test_feats, factor_panel)


def gram_kernel(at_ref, got_ref, train_ref, mine_ref, theirs_ref):
    l, c, h = at_ref[0], at_ref[1], at_ref[2]
    place = lax.broadcasted_iota(jnp.int32, (256, 256), 0)
    column = lax.broadcasted_iota(jnp.int32, (256, 256), 1)
    yx, l_of, c_of = (place >> 3) & 15, (l + (place >> 1)) & 3, (c + (place >> 7)) & 1
    wanted = (yx << 4) + (l_of << 2) + (c_of << 1) + (place & 1)
    choose = jnp.where(wanted == column, 1.0, 0.0).astype(BF16)
    panel = jnp.where(h == 0, train_ref[:, :W].astype(F32), got_ref[...].astype(F32)).astype(BF16)
    panel = lax.dot_general(choose, panel, (((1,), (1,)), ((), ())), preferred_element_type=F32)
    panel = panel.astype(BF16)
    for i in range(8):
        term = jnp.dot(panel, train_ref[:, 512 * i : 512 * i + 512], preferred_element_type=F32)
        blocks = [term[:, 128 * t : 128 * t + 128].reshape(32, 8, 128) for t in range(4)]
        term = jnp.concatenate(blocks, axis=1)
        mine_ref[:, 32 * i : 32 * i + 32, :] = term[:16]
        theirs_ref[:, 32 * i : 32 * i + 32, :] = term[16:].astype(BF16)


def gram_terms(at, got, train_feats):
    return pl.pallas_call(
        gram_kernel,
        in_specs=[pl.BlockSpec(memory_space=pltpu.SMEM), whole(), whole()],
        out_specs=[whole()] * 2,
        out_shape=[
            jax.ShapeDtypeStruct((16, 256, 128), F32),
            jax.ShapeDtypeStruct((16, 256, 128), BF16),
        ],
        compiler_params=params(16),
        cost_estimate=cost(2 * 256 * 512 * 4096, 7 * MIB),
        name="gram_terms",
    )(at, got, train_feats)


def halves_kernel(keep_ref, got_ref, out_ref):
    proj = (keep_ref[...] + got_ref[...].astype(F32)).astype(BF16)
    for dest in range(8):
        out_ref[dest] = proj[:, 128 * (dest % 2) : 128 * (dest % 2) + 128]


def sum_halves(keep, got):
    return pl.pallas_call(
        halves_kernel,
        in_specs=[whole()] * 2,
        out_specs=whole(),
        out_shape=jax.ShapeDtypeStruct((8, 64, 128), BF16),
        compiler_params=params(8),
        cost_estimate=cost(1 << 16, MIB // 4),
        name="sum_halves",
    )(keep, got)


def spread_kernel(parts_ref, out_ref):
    proj = parts_ref[...].astype(F32).reshape(4, 128, 128)
    proj = jnp.concatenate([proj[l].T for l in range(4)], axis=0).astype(BF16)
    for dest in range(16):
        out_ref[dest] = proj


def spread(parts):
    return pl.pallas_call(
        spread_kernel,
        in_specs=[whole()],
        out_specs=whole(),
        out_shape=jax.ShapeDtypeStruct((16, 512, 128), BF16),
        compiler_params=params(8),
        cost_estimate=cost(MIB, 2 * MIB),
        name="spread",
    )(parts)


def cores_kernel(mine_ref, got_ref, out_ref):
    out_ref[...] = (mine_ref[...] + got_ref[...].astype(F32)).astype(BF16)


def sum_cores(mine, got):
    return pl.pallas_call(
        cores_kernel,
        in_specs=[whole()] * 2,
        out_specs=whole(),
        out_shape=jax.ShapeDtypeStruct((16, 256, 128), BF16),
        compiler_params=params(8),
        cost_estimate=cost(MIB // 2, 4 * MIB),
        name="sum_cores",
    )(mine, got)


def fold_kernel(in_ref, own_ref, a_ref, b_ref, d_ref, sum_ref):
    total = in_ref[0].astype(F32)
    for s in range(1, 16):
        total = total + in_ref[s].astype(F32)
    sum_ref[...] = total
    for step, ref in enumerate((own_ref, a_ref, b_ref, d_ref)):
        for j in range(2):
            rows = sum_ref[pl.ds(2 * step + j, 32, stride=8), :]
            ref[32 * j : 32 * j + 32, :] = rows.astype(ref.dtype)


def fold(rows):
    return pl.pallas_call(
        fold_kernel,
        in_specs=[whole()],
        out_specs=[whole()] * 4,
        out_shape=[jax.ShapeDtypeStruct((64, 128), F32)] + [jax.ShapeDtypeStruct((64, 128), BF16)] * 3,
        scratch_shapes=[pltpu.VMEM((256, 128), F32)],
        compiler_params=params(8),
        cost_estimate=cost(MIB // 2, MIB),
        name="fold",
    )(rows)


def train_kernel(at_ref, train_ref, factor_ref, keep_ref, give_ref, sum_ref):
    for n in range(4):
        rows = slice(128 * n, 128 * n + 128)
        sum_ref[rows, :] = jnp.dot(train_ref[rows, :], factor_ref[...], preferred_element_type=F32)
    h = at_ref[2]
    keep_ref[...] = sum_ref[pl.ds(pl.multiple_of(256 * h, 256), 256), :]
    give_ref[...] = sum_ref[pl.ds(pl.multiple_of(256 - 256 * h, 256), 256), :].astype(BF16)


def train_parts(at, train_feats, factor_panel):
    return pl.pallas_call(
        train_kernel,
        in_specs=[pl.BlockSpec(memory_space=pltpu.SMEM), whole(), whole()],
        out_specs=[whole()] * 2,
        out_shape=[jax.ShapeDtypeStruct((256, 256), F32), jax.ShapeDtypeStruct((256, 256), BF16)],
        scratch_shapes=[pltpu.VMEM((512, 256), F32)],
        compiler_params=params(8),
        cost_estimate=cost(2 * 512 * 4096 * 256, 7 * MIB),
        name="train_parts",
    )(at, train_feats, factor_panel)


def scores_kernel(at_ref, keep_ref, got_ref, own_ref, other_ref, out_ref, made_ref, sem):
    c = at_ref[1]
    proj = keep_ref[...] + got_ref[...].astype(F32)
    low, high = proj[:, :128], proj[:, 128:]
    proj = jnp.concatenate([jnp.where(c == 0, low, high), jnp.where(c == 0, high, low)], axis=1)
    proj = proj.astype(BF16)
    copies = []
    for n in range(32):
        tests = jnp.concatenate(
            [
                jnp.concatenate(
                    [
                        ref[n // 2, 256 * (n % 2) + 128 * t : 256 * (n % 2) + 128 * t + 128, :]
                        for t in range(2)
                    ],
                    axis=1,
                )
                for ref in (own_ref, other_ref)
            ],
            axis=0,
        )
        product = jnp.dot(proj, tests, preferred_element_type=F32)
        made_ref[:, 256 * n : 256 * n + 256] = (product * (1.0 / math.sqrt(256))).astype(BF16)
        if n % 4 == 3:
            done = pl.ds(256 * (n - 3), 1024)
            copies.append(
                pltpu.make_async_copy(made_ref.at[:, done], out_ref.at[:, done], sem.at[n // 4])
            )
            copies[-1].start()
    for copy in copies:
        copy.wait()


def scores_of(at, keep, got, own, other):
    return pl.pallas_call(
        scores_kernel,
        in_specs=[pl.BlockSpec(memory_space=pltpu.SMEM)] + [whole()] * 4,
        out_specs=anywhere(),
        out_shape=jax.ShapeDtypeStruct((256, 8192), BF16),
        scratch_shapes=[pltpu.VMEM((256, 8192), BF16), pltpu.SemaphoreType.DMA((8,))],
        compiler_params=params(16),
        cost_estimate=cost(1 << 30, 8 * MIB),
        name="scores",
    )(at, keep, got, own, other)


def local(train_feats, test_feats, factor_panel):
    at = jnp.stack([lax.axis_index(a) for a in ("l", "c", "h")]).astype(jnp.int32)

    test_keep, test_give = test_parts(test_feats, factor_panel)
    parts = sum_halves(test_keep, lax.ppermute(test_give, AXES, OTHER_HALF))
    keep, give = train_parts(at, train_feats, factor_panel)
    parts, give = lax.optimization_barrier((parts, give))
    parts = lax.all_to_all(parts, ("l", "c"), 0, 0, tiled=True)
    tests = spread(parts)

    feats, _ = lax.optimization_barrier((train_feats, tests))
    sent = lax.ppermute(feats[:, :W], AXES, TO_SECOND_HALF)
    sent, give, _ = lax.optimization_barrier((sent, give, tests))
    got = lax.ppermute(give, AXES, OTHER_HALF)
    mine, theirs = gram_terms(at, sent, train_feats)
    rows = sum_cores(mine, lax.ppermute(theirs, AXES, OTHER_CORE))
    tests = lax.all_to_all(tests, ("y", "x"), 0, 0, tiled=True)
    tests, rows = lax.optimization_barrier((tests, rows))

    other = lax.ppermute(tests, AXES, OTHER_CORE)
    rows = lax.all_to_all(rows, ("y", "x"), 0, 0, tiled=True)
    scores = scores_of(at, keep, got, tests, other)
    rows, scores = lax.optimization_barrier((rows, scores))
    total, *sums = fold(rows)
    for d, block in enumerate(sums, 1):
        total = total + lax.ppermute(block, AXES, ALONG[d]).astype(F32)
    gram_panel = total.reshape(2, 4096) / 65536
    return (gram_panel, scores)


def solution(mesh):
    fine = Mesh(mesh.devices.reshape(SIZES), AXES)
    seg = ("y", "x", "l", "c")
    in_specs = (P(seg, "h"), P(seg, "h"), P("h", None))
    out_specs = (P(seg, "h"), P((*seg, "h"), None))
    return jax.shard_map(local, mesh=fine, in_specs=in_specs, out_specs=out_specs, check_vma=False)
```
